256 devices in a mesh: chan: 32 (over x, z_lo, y), ablk: 8 (over z_hi, core).
Axes of the slice: x: 4, y: 4, z: 8 (z_hi: 4, z_lo: 2; z = z_hi * 2 + z_lo), core: 2. Of those that a mesh axis runs over, the one named last changes fastest.
Arguments:
- voltages: int32 [2, 4096, 32, 512], P(None, ('chan', 'ablk')), may hold values from -7 to 7
- complex_gains: float32 [2, 4096, 32], P(None, ('chan', 'ablk')), may hold values from -4 to 4
Outputs:
- visibilities: float32 [32, 2, 18432, 512], P('chan', None, 'ablk')
The draws below stay inside these ranges and needn't reach their ends.
All inputs are finite; a program needn't handle non-finite values.
Results may differ from the reference program's by a relative error of at most 0.0034.
Values may be sent and summed in bfloat16 or wider, within the bound.
A program may use at most 64 MiB of HBM per device.

```python
import jax
import jax.numpy as jnp
from jax import lax

INPUTS = 4096
TIME = 512
CHANNELS = 32
INP_DEV = 16
BLK = 512
N_CHAN = 32
N_ABLK = 8


def set_ends(drawn, own_key, least, largest):
    longest = drawn.shape.index(max(drawn.shape))
    spots = []
    for shift in (0, 1):
        where = [jax.random.randint(jax.random.fold_in(own_key, axis), (), 0, length) for axis, length in enumerate(drawn.shape)]
        where[longest] = (where[longest] + shift) % drawn.shape[longest]
        spots.append(tuple(where))
    return drawn.at[spots[0]].set(least).at[spots[1]].set(largest)


def level_of(rng, dims, shards, least, high):
    level = 1.0
    for position, blocks in shards:
        heights = jax.random.uniform(jax.random.fold_in(jax.random.fold_in(rng, 6), position), (blocks,), jnp.float32, least / len(shards), high / len(shards))
        level = level * jnp.repeat(jnp.exp(heights), dims[position] // blocks).reshape((-1,) + (1,) * (len(dims) - 1 - position))
    return level


def scatter_about(stream_key, dims, spread, bound, split=(), kind=jnp.bfloat16):
    factor_of = level_of(stream_key, dims, split, -0.22, 0.18) if split else 1.0
    entries = jax.random.normal(stream_key, dims, jnp.float32) * spread * factor_of
    return jnp.minimum(jnp.maximum(entries, -bound), bound).astype(kind)


def setup_inputs(seed: int = 0) -> dict:
    keys = jax.random.split(jax.random.key(seed), 3)
    voltages = set_ends(jax.random.randint(keys[0], (2, INPUTS, CHANNELS, TIME), -7, 8), jax.random.fold_in(keys[0], 1), -7, 7).astype(jnp.int32)
    complex_gains = scatter_about(keys[1], (2, INPUTS, CHANNELS), 0.7, 4.0, ((1, 256),), jnp.float32)
    return {"voltages": voltages, "complex_gains": complex_gains}


def block_pair(left_rows, right_rows, norm_factor):
    channel_count = left_rows.shape[0]
    row_count = left_rows.shape[2]
    block_rows = right_rows.shape[2]
    samples = left_rows.shape[3]
    left_flat = left_rows.reshape(channel_count, 2 * row_count, samples).astype(jnp.float32)
    right_flat = right_rows.reshape(channel_count, 2 * block_rows, samples).astype(jnp.float32)
    products = jnp.einsum("cit,cjt->cij", left_flat, right_flat, precision=lax.Precision.HIGHEST)
    products = products.reshape(channel_count, 2, row_count, 2, block_rows)
    real_part = products[:, 0, :, 0] + products[:, 1, :, 1]
    imag_part = products[:, 1, :, 0] - products[:, 0, :, 1]
    return jnp.stack((real_part, imag_part), axis=1) * norm_factor


def reference(voltages, complex_gains):
    volt_re = voltages[0].astype(jnp.float32)
    volt_im = voltages[1].astype(jnp.float32)
    gain_re = complex_gains[0][:, :, None]
    gain_im = complex_gains[1][:, :, None]
    calibrated = jnp.stack((gain_re * volt_re - gain_im * volt_im, gain_re * volt_im + gain_im * volt_re), axis=0).astype(jnp.bfloat16)
    blocks = calibrated.reshape(2, N_CHAN, N_ABLK, INP_DEV, CHANNELS, TIME)
    blocks = jnp.transpose(blocks, (4, 2, 0, 1, 3, 5)).reshape(CHANNELS, N_ABLK, 2, BLK, TIME)
    norm_factor = 1.0 / (4.0 * TIME)
    midway = N_ABLK // 2

    def one_channel(channel_blocks):
        stacked = []
        for device in range(N_ABLK):
            local_block = channel_blocks[device][None]
            pieces = [block_pair(local_block, local_block, norm_factor)]
            for offset in range(1, midway + 1):
                partner = channel_blocks[(device + offset) % N_ABLK][None]
                if offset < midway:
                    pieces.append(block_pair(local_block, partner, norm_factor))
                elif device < midway:
                    pieces.append(block_pair(local_block[:, :, : BLK // 2], partner, norm_factor))
                else:
                    pieces.append(block_pair(partner[:, :, BLK // 2:], local_block, norm_factor))
            stacked.append(jnp.concatenate(pieces, axis=2))
        return jnp.concatenate(stacked, axis=2)[0]

    return lax.map(one_channel, blocks)
```

```python
import functools

import jax
import jax.numpy as jnp
from jax import lax
from jax.experimental import pallas as pl
from jax.experimental.pallas import tpu as pltpu
from jax.sharding import PartitionSpec as P

MESH = pl.DeviceIdType.MESH

SIDE = 4
PEERS = SIDE * SIDE
GROUPS = 4
ROWS = 16
LANES = 128
PLUS = 5


def coordinates():
    chan, ablk = lax.axis_index("chan"), lax.axis_index("ablk")
    x, parity, y = chan // 8, (chan // 4) % 2, chan % 4
    return x, y, (ablk // 2) * 2 + parity, ablk % 2


def device(x, y, z, core):
    z = (z + 8) % 8
    return x * 8 + (z % 2) * 4 + y, (z // 2) * 2 + core


def peer(x, y, i):
    return (x + i % SIDE) % SIDE, (y + i // SIDE + i % SIDE) % SIDE


def gather_kernel(volt, gain, blocks, cal, other, stash, block_sem, other_sem, stash_sem, twin_sem, send_sem):
    x, y, z, core = coordinates()
    parity = z % 2
    channels = cal.shape[0]
    lane_tiles = cal.shape[3] // LANES
    step = channels * lane_tiles
    home = z + 1 - 2 * parity
    me_c = x * 8 + parity * 4 + y

    barrier = pltpu.get_barrier_semaphore()

    def greet(i, carry):
        px, py = peer(x, y, i)
        pl.semaphore_signal(barrier, inc=1, device_id=device(px, py, z, core), device_id_type=MESH)
        return carry

    lax.fori_loop(1, PEERS, greet, 0)
    for source in (z + 2, z - 2, home, z - 3 + 4 * parity):
        pl.semaphore_signal(barrier, inc=1, device_id=device(x, y, source, core), device_id_type=MESH)
    pl.semaphore_signal(barrier, inc=1, device_id=device(x, y, z, 1 - core), device_id_type=MESH)

    for f in range(channels):
        gain_re = jnp.broadcast_to(gain[0, :, f : f + 1], (ROWS, LANES))
        gain_im = jnp.broadcast_to(gain[1, :, f : f + 1], (ROWS, LANES))
        for t in range(lane_tiles):
            start = (f // 8 * lane_tiles + t) * 8 + f % 8
            volt_re = volt[pl.ds(start, ROWS, stride=step), :].astype(jnp.float32)
            volt_im = volt[pl.ds(ROWS * step + start, ROWS, stride=step), :].astype(jnp.float32)
            cal[f, 0, :, t * LANES : (t + 1) * LANES] = (gain_re * volt_re - gain_im * volt_im).astype(jnp.bfloat16)
            cal[f, 1, :, t * LANES : (t + 1) * LANES] = (gain_re * volt_im + gain_im * volt_re).astype(jnp.bfloat16)

    pl.semaphore_wait(barrier, PEERS + 4)

    def send(src, dst, kind, sem, to):
        pltpu.make_async_remote_copy(
            src_ref=src, dst_ref=dst, send_sem=send_sem.at[kind], recv_sem=sem, device_id=to, device_id_type=MESH
        ).start()

    def arrived(ref, sem):
        pltpu.make_async_copy(ref, ref, sem).wait()

    def place(i, p):
        px, py = peer(x, y, i)
        return px * 8 + p * 4 + py

    def channel_of(px, py, p):
        return px * 8 + p * 4 + py

    pltpu.make_async_copy(cal.at[me_c], blocks.at[0, :, me_c], block_sem.at[0, 0]).start()
    pltpu.make_async_copy(cal.at[channel_of(x, y, 1 - parity)], other.at[:, 0], other_sem.at[0]).start()

    def scatter(i, carry):
        px, py = (x + SIDE - i % SIDE) % SIDE, (y + 2 * SIDE - i // SIDE - i % SIDE) % SIDE
        to = device(px, py, z, core)
        send(cal.at[channel_of(px, py, parity)], blocks.at[0, :, me_c], 0, block_sem.at[0, i], to)
        send(cal.at[channel_of(px, py, 1 - parity)], other.at[:, i], 1, other_sem.at[i], to)
        return carry

    lax.fori_loop(1, PEERS, scatter, 0)

    def share(slot, c):
        def go():
            send(
                blocks.at[2 * slot, :, c],
                blocks.at[2 * (slot - 1 + core) + 1, :, c],
                2,
                twin_sem.at[slot - 1 + core],
                device(x, y, z, 1 - core),
            )

        if isinstance(slot, int) and slot == 1:
            go()
        else:
            pl.when((slot == 1) | (slot == 2 - 2 * core))(go)

    up, down = device(x, y, z + 2, core), device(x, y, z - 2, core)

    def direct(i, carry):
        c = place(i, parity)
        arrived(blocks.at[0, :, c], block_sem.at[0, i])

        @pl.when(i < PLUS)
        def _():
            send(blocks.at[0, :, c], stash.at[:, i], 3, stash_sem.at[i], up)

        @pl.when(i >= PLUS)
        def _():
            send(blocks.at[0, :, c], blocks.at[2, :, c], 4, block_sem.at[1, i], down)

        share(0, c)
        arrived(other.at[:, i], other_sem.at[i])
        send(other.at[:, i], blocks.at[0, :, c], 5, block_sem.at[0, PEERS + i], device(x, y, home, core))
        send(
            other.at[:, i],
            blocks.at[2 + 2 * parity, :, c],
            6,
            block_sem.at[1 + parity, PEERS + i],
            device(x, y, z - 1 + 4 * parity, core),
        )
        return carry

    lax.fori_loop(0, PEERS, direct, 0)

    def lift(i, carry):
        arrived(stash.at[:, i], stash_sem.at[i])
        send(stash.at[:, i], blocks.at[4, :, place(i, parity)], 7, block_sem.at[2, i], up)
        return carry

    lax.fori_loop(0, PLUS, lift, 0)

    def relay(i, carry):
        mine, theirs = place(i, parity), place(i, 1 - parity)
        arrived(blocks.at[0, :, theirs], block_sem.at[0, PEERS + i])
        share(0, theirs)
        first = 2 - parity
        arrived(blocks.at[2 * first, :, theirs], block_sem.at[first, PEERS + i])
        send(
            blocks.at[2 * first, :, theirs],
            blocks.at[2 * (1 + parity), :, theirs],
            8,
            block_sem.at[1 + parity, PEERS + i],
            device(x, y, z + 2 - 4 * parity, core),
        )
        share(first, theirs)

        @pl.when(i < PLUS)
        def _():
            arrived(blocks.at[4, :, mine], block_sem.at[2, i])
            send(blocks.at[4, :, mine], blocks.at[2, :, mine], 9, block_sem.at[1, i], up)
            share(2, mine)

        @pl.when(i >= PLUS)
        def _():
            arrived(blocks.at[2, :, mine], block_sem.at[1, i])
            send(blocks.at[2, :, mine], blocks.at[4, :, mine], 10, block_sem.at[2, i], down)
            share(1, mine)

        return carry

    lax.fori_loop(0, PEERS, relay, 0)

    def last(i, carry):
        mine, theirs = place(i, parity), place(i, 1 - parity)
        second = 1 + parity
        arrived(blocks.at[2 * second, :, theirs], block_sem.at[second, PEERS + i])
        share(second, theirs)

        @pl.when(i < PLUS)
        def _():
            arrived(blocks.at[2, :, mine], block_sem.at[1, i])
            share(1, mine)

        @pl.when(i >= PLUS)
        def _():
            arrived(blocks.at[4, :, mine], block_sem.at[2, i])
            share(2, mine)

        return carry

    lax.fori_loop(0, PEERS, last, 0)

    def sent(kind, count, slot=0):
        ref = blocks.at[slot, :, pl.ds(0, count)]
        pltpu.make_async_copy(ref, ref, send_sem.at[kind]).wait()

    for kind, count in enumerate((15, 15, 64, PLUS, 11, 16, 16, PLUS, 16, PLUS, 11)):
        if kind != 2:
            sent(kind, count)
    pair = blocks.at[pl.ds(0, 2)]
    pltpu.make_async_copy(pair, pair, send_sem.at[2]).wait()
    arrived(blocks.at[1], twin_sem.at[0])
    arrived(blocks.at[3], twin_sem.at[1])


def pair_kernel(left_ref, right_ref, out_ref, *, scale):
    left_re, left_im = left_ref[0, 0], left_ref[0, 1]
    right_re, right_im = right_ref[0, 0], right_ref[0, 1]

    def dot(a, b):
        return lax.dot_general(a, b, (((1,), (1,)), ((), ())), preferred_element_type=jnp.float32)

    out_ref[0] = (dot(left_re, right_re) + dot(left_im, right_im)) * scale
    out_ref[1] = (dot(left_im, right_re) - dot(left_re, right_im)) * scale


def body(voltages, complex_gains):
    parts, rows, channels, samples = voltages.shape
    tiles = voltages.reshape(parts, rows, channels // 8, 8, samples // LANES, LANES).transpose(0, 1, 2, 4, 3, 5)
    blocks = pl.pallas_call(
        gather_kernel,
        out_shape=jax.ShapeDtypeStruct((5, parts, 32, rows, samples), jnp.bfloat16),
        in_specs=[pl.BlockSpec(memory_space=pltpu.VMEM)] * 2,
        out_specs=pl.BlockSpec(memory_space=pltpu.VMEM),
        scratch_shapes=[
            pltpu.VMEM((channels, parts, rows, samples), jnp.bfloat16),
            pltpu.VMEM((parts, PEERS, rows, samples), jnp.bfloat16),
            pltpu.VMEM((parts, PLUS, rows, samples), jnp.bfloat16),
            pltpu.SemaphoreType.DMA((3, 2 * PEERS)),
            pltpu.SemaphoreType.DMA((PEERS,)),
            pltpu.SemaphoreType.DMA((PLUS,)),
            pltpu.SemaphoreType.DMA((2,)),
            pltpu.SemaphoreType.DMA((11,)),
        ],
        compiler_params=pltpu.CompilerParams(
            collective_id=0, has_side_effects=True, vmem_limit_bytes=40 * 1024 * 1024
        ),
        name="gather",
    )(tiles.reshape(-1, LANES), complex_gains)

    size = 32 * rows
    half = size // 2
    blocks = blocks.reshape(5, parts, size, samples)
    steps = 9
    upper = lax.axis_index("ablk") >= 4

    def left_index(j, flag):
        return (jnp.where((j == 8) & (flag[0] == 1), 4, 0), 0, jnp.where(j == 8, flag[0], j % 2), 0)

    def right_index(j, flag):
        return (jnp.where((j == 8) & (flag[0] == 1), 0, j // 2), 0, 0, 0)

    out = pl.pallas_call(
        functools.partial(pair_kernel_flagged, scale=1.0 / (4.0 * samples)),
        out_shape=jax.ShapeDtypeStruct((parts, steps * half, size), jnp.float32),
        grid_spec=pltpu.PrefetchScalarGridSpec(
            num_scalar_prefetch=1,
            grid=(steps,),
            in_specs=[
                pl.BlockSpec((1, parts, half, samples), left_index),
                pl.BlockSpec((1, parts, size, samples), right_index),
            ],
            out_specs=pl.BlockSpec((parts, half, size), lambda j, flag: (0, j, 0)),
        ),
        compiler_params=pltpu.CompilerParams(vmem_limit_bytes=40 * 1024 * 1024),
        name="pairs",
    )(upper.astype(jnp.int32)[None], blocks, blocks)
    return out[None]


def pair_kernel_flagged(flag, left_ref, right_ref, out_ref, *, scale):
    del flag
    pair_kernel(left_ref, right_ref, out_ref, scale=scale)


def solution(mesh):
    in_specs = (P(None, ("chan", "ablk"), None, None), P(None, ("chan", "ablk"), None))
    out_specs = P("chan", None, "ablk", None)
    return jax.shard_map(body, mesh=mesh, in_specs=in_specs, out_specs=out_specs, check_vma=False)
```

```python
import functools

import jax
import jax.numpy as jnp
from jax import lax
from jax.experimental import pallas as pl
from jax.experimental.pallas import tpu as pltpu
from jax.sharding import PartitionSpec as P

MESH = pl.DeviceIdType.MESH

SIDE = 4
PEERS = SIDE * SIDE
ROWS = 16
LANES = 128
OCTET = 8
PLUS = 5
DELAY = 8
EARLY = 4
LIFT = 8


def coordinates():
    chan, ablk = lax.axis_index("chan"), lax.axis_index("ablk")
    return chan // 8, chan % 4, (ablk // 2) * 2 + (chan // 4) % 2, ablk % 2


def device(x, y, z, core):
    z = (z + 8) % 8
    return x * 8 + (z % 2) * 4 + y, (z // 2) * 2 + core


def gather_kernel(
    volt, gain_hbm, blocks, raw, gain, cal, other, stash,
    raw_sem, gain_sem, block_sem, other_sem, stash_sem, twin_sem, send_sem,
):
    x, y, z, core = coordinates()
    parity = z % 2
    home = z + 1 - 2 * parity
    lane_tiles = cal.shape[3] // LANES
    step, pitch = OCTET * lane_tiles, raw.shape[2]
    me_c = x * 8 + parity * 4 + y

    gain_copy = pltpu.make_async_copy(gain_hbm, gain, gain_sem)
    gain_copy.start()
    raw_copies = []
    for j in range(SIDE):
        target = (x + SIDE - j) % SIDE
        raw_copies.append(pltpu.make_async_copy(volt.at[:, target], raw.at[j, :, pl.ds(0, step)], raw_sem.at[j]))
        raw_copies[-1].start()

    barrier = pltpu.get_barrier_semaphore()

    def greet(i, carry):
        to = device((x + i // SIDE) % SIDE, (y + i % SIDE) % SIDE, z, core)
        pl.semaphore_signal(barrier, inc=1, device_id=to, device_id_type=MESH)
        return carry

    lax.fori_loop(1, PEERS, greet, 0)
    for source in (z + 2, z - 2, home, z - 3 + 4 * parity):
        pl.semaphore_signal(barrier, inc=1, device_id=device(x, y, source, core), device_id_type=MESH)
    pl.semaphore_signal(barrier, inc=1, device_id=device(x, y, z, 1 - core), device_id_type=MESH)

    def send(src, dst, kind, sem, to):
        pltpu.make_async_remote_copy(
            src_ref=src, dst_ref=dst, send_sem=send_sem.at[kind], recv_sem=sem, device_id=to, device_id_type=MESH
        ).start()

    def arrived(ref, sem):
        pltpu.make_async_copy(ref, ref, sem).wait()

    def place(i, p):
        return (x + i // SIDE) % SIDE * 8 + p * 4 + (y + i % SIDE) % SIDE

    def share(slot, c):
        def go():
            to = slot - 1 + core
            send(blocks.at[2 * slot, :, c], blocks.at[2 * to + 1, :, c], 2, twin_sem.at[to], device(x, y, z, 1 - core))

        if isinstance(slot, int) and slot == 1:
            go()
        else:
            pl.when((slot == 1) | (slot == 2 - 2 * core))(go)

    up, down = device(x, y, z + 2, core), device(x, y, z - 2, core)

    def direct(i, carry):
        c = place(i, parity)
        arrived(blocks.at[0, :, c], block_sem.at[0, i])

        @pl.when(i < PLUS)
        def _():
            send(blocks.at[0, :, c], stash.at[:, i], 3, stash_sem.at[i], up)

        @pl.when(i >= PLUS)
        def _():
            send(blocks.at[0, :, c], blocks.at[2, :, c], 4, block_sem.at[1, i], down)

        arrived(other.at[:, i], other_sem.at[i])
        send(
            other.at[:, i],
            blocks.at[2 + 2 * parity, :, c],
            6,
            block_sem.at[1 + parity, PEERS + i],
            device(x, y, z - 1 + 4 * parity, core),
        )
        send(other.at[:, i], blocks.at[0, :, c], 5, block_sem.at[0, PEERS + i], device(x, y, home, core))
        share(0, c)

        @pl.when((i >= LIFT) & (i < LIFT + PLUS))
        def _():
            k = i - LIFT
            arrived(stash.at[:, k], stash_sem.at[k])
            send(stash.at[:, k], blocks.at[4, :, place(k, parity)], 7, block_sem.at[2, k], up)

        return carry

    gain_copy.wait()
    for j in range(SIDE):
        target = (x + SIDE - j) % SIDE
        raw_copies[j].wait()
        octet = raw.at[j].reshape(2 * ROWS * pitch, LANES)
        gain_re, gain_im = gain[0, :, :OCTET], gain[1, :, :OCTET]
        for o in range(1, SIDE):
            gain_re = jnp.where(target == o, gain[0, :, o * OCTET : (o + 1) * OCTET], gain_re)
            gain_im = jnp.where(target == o, gain[1, :, o * OCTET : (o + 1) * OCTET], gain_im)
        for s in range(OCTET):
            g_re = jnp.broadcast_to(gain_re[:, s : s + 1], (ROWS, LANES))
            g_im = jnp.broadcast_to(gain_im[:, s : s + 1], (ROWS, LANES))
            f = target * OCTET + s
            for t in range(lane_tiles):
                start = t * OCTET + s
                v_re = octet[pl.ds(start, ROWS, stride=pitch), :].astype(jnp.float32)
                v_im = octet[pl.ds(ROWS * pitch + start, ROWS, stride=pitch), :].astype(jnp.float32)
                cal[f, 0, :, t * LANES : (t + 1) * LANES] = (g_re * v_re - g_im * v_im).astype(jnp.bfloat16)
                cal[f, 1, :, t * LANES : (t + 1) * LANES] = (g_re * v_im + g_im * v_re).astype(jnp.bfloat16)

        if j == 0:
            pl.semaphore_wait(barrier, PEERS + 4)
            pltpu.make_async_copy(cal.at[me_c], blocks.at[0, :, me_c], block_sem.at[0, 0]).start()
            pltpu.make_async_copy(cal.at[x * 8 + (1 - parity) * 4 + y], other.at[:, 0], other_sem.at[0]).start()

        def scatter(k, carry, j=j, target=target):
            row = (y + SIDE - k) % SIDE
            to = device(target, row, z, core)
            i = j * SIDE + k
            send(cal.at[target * 8 + parity * 4 + row], blocks.at[0, :, me_c], 0, block_sem.at[0, i], to)
            send(cal.at[target * 8 + (1 - parity) * 4 + row], other.at[:, i], 1, other_sem.at[i], to)
            return carry

        lax.fori_loop(1 if j == 0 else 0, SIDE, scatter, 0)
        if j < EARLY:
            direct(j, 0)

    first, second = 2 - parity, 1 + parity

    def relay(i, carry):
        mine, theirs = place(i, parity), place(i, 1 - parity)
        arrived(blocks.at[2 * first, :, theirs], block_sem.at[first, PEERS + i])
        send(
            blocks.at[2 * first, :, theirs],
            blocks.at[2 * second, :, theirs],
            8,
            block_sem.at[second, PEERS + i],
            device(x, y, z + 2 - 4 * parity, core),
        )
        share(first, theirs)

        @pl.when(i >= PLUS)
        def _():
            arrived(blocks.at[2, :, mine], block_sem.at[1, i])
            send(blocks.at[2, :, mine], blocks.at[4, :, mine], 10, block_sem.at[2, i], down)
            share(1, mine)

        @pl.when((i >= LIFT) & (i < LIFT + PLUS))
        def _():
            k = i - LIFT
            lifted = place(k, parity)
            arrived(blocks.at[4, :, lifted], block_sem.at[2, k])
            send(blocks.at[4, :, lifted], blocks.at[2, :, lifted], 9, block_sem.at[1, k], up)
            share(2, lifted)

        return carry

    def both(i, carry):
        direct(i, 0)

        @pl.when(i >= DELAY)
        def _():
            relay(i - DELAY, 0)

        return carry

    lax.fori_loop(EARLY, PEERS, both, 0)

    lax.fori_loop(PEERS - DELAY, PEERS, relay, 0)

    def last(i, carry):
        mine, theirs = place(i, parity), place(i, 1 - parity)
        arrived(blocks.at[0, :, theirs], block_sem.at[0, PEERS + i])
        share(0, theirs)
        arrived(blocks.at[2 * second, :, theirs], block_sem.at[second, PEERS + i])
        share(second, theirs)

        @pl.when(i < PLUS)
        def _():
            arrived(blocks.at[2, :, mine], block_sem.at[1, i])
            share(1, mine)

        @pl.when(i >= PLUS)
        def _():
            arrived(blocks.at[4, :, mine], block_sem.at[2, i])
            share(2, mine)

        return carry

    lax.fori_loop(0, PEERS, last, 0)

    def sent(kind, count):
        ref = blocks.at[0, :, pl.ds(0, count)]
        pltpu.make_async_copy(ref, ref, send_sem.at[kind]).wait()

    rest = PEERS - PLUS
    for kind, count in ((0, 15), (1, 15), (3, PLUS), (4, rest), (5, 16), (6, 16), (7, PLUS), (8, 16), (9, PLUS), (10, rest)):
        sent(kind, count)
    pair = blocks.at[pl.ds(0, 2)]
    pltpu.make_async_copy(pair, pair, send_sem.at[2]).wait()
    arrived(blocks.at[1], twin_sem.at[0])
    arrived(blocks.at[3], twin_sem.at[1])


def product(left, right):
    rows = jnp.concatenate(
        (jnp.concatenate((left[0], left[1]), axis=1), jnp.concatenate((left[1], -left[0]), axis=1)), axis=0
    )
    columns = jnp.concatenate((right[0], right[1]), axis=1)
    return lax.dot_general(rows, columns, (((1,), (1,)), ((), ())), preferred_element_type=jnp.float32)


def pairs_kernel(blocks, out, made, sem, *, scale):
    upper = (lax.axis_index("ablk") >= 4).astype(jnp.int32)
    steps, parts, half, size = made.shape

    def copy(j):
        return pltpu.make_async_copy(made.at[j], out.at[:, pl.ds(j * half, half)], sem.at[j])

    def make(j):
        if j < steps - 1:
            left, right = blocks[0, :, j % 2 * half : (j % 2 + 1) * half, :], blocks[j // 2]
        else:
            left = blocks[4 * upper, :, pl.ds(pl.multiple_of(upper * half, half), half), :]
            right = blocks[4 - 4 * upper]
        made[j] = (product(left, right) * scale).reshape(parts, half, size)
        copy(j).start()

    for j in range(steps):
        make(j)

    for j in range(steps):
        copy(j).wait()


def body(voltages, complex_gains):
    parts, rows, channels, samples = voltages.shape
    lane_tiles = samples // LANES
    octets = channels // OCTET
    tiles = voltages.reshape(parts, rows, octets, OCTET, lane_tiles, LANES).transpose(0, 1, 2, 4, 3, 5)
    tiles = tiles.reshape(parts * rows, octets, lane_tiles * OCTET, LANES)
    blocks = pl.pallas_call(
        gather_kernel,
        out_shape=pltpu.VMEM((5, parts, 32, rows, samples), jnp.bfloat16),
        in_specs=[pl.BlockSpec(memory_space=pltpu.HBM)] * 2,
        out_specs=pl.BlockSpec(memory_space=pltpu.VMEM),
        scratch_shapes=[
            pltpu.VMEM((octets, parts * rows, lane_tiles * OCTET + 8, LANES), jnp.int32),
            pltpu.VMEM((parts, rows, channels), jnp.float32),
            pltpu.VMEM((channels, parts, rows, samples), jnp.bfloat16),
            pltpu.VMEM((parts, PEERS, rows, samples), jnp.bfloat16),
            pltpu.VMEM((parts, PLUS, rows, samples), jnp.bfloat16),
            pltpu.SemaphoreType.DMA((SIDE,)),
            pltpu.SemaphoreType.DMA,
            pltpu.SemaphoreType.DMA((3, 2 * PEERS)),
            pltpu.SemaphoreType.DMA((PEERS,)),
            pltpu.SemaphoreType.DMA((PLUS,)),
            pltpu.SemaphoreType.DMA((2,)),
            pltpu.SemaphoreType.DMA((11,)),
        ],
        compiler_params=pltpu.CompilerParams(
            collective_id=0, has_side_effects=True, vmem_limit_bytes=40 * 1024 * 1024
        ),
        name="gather",
    )(*(pltpu.with_memory_space_constraint(a, pltpu.HBM) for a in (tiles, complex_gains)))

    size = 32 * rows
    half = size // 2
    steps = 9
    out = pl.pallas_call(
        functools.partial(pairs_kernel, scale=1.0 / (4.0 * samples)),
        out_shape=jax.ShapeDtypeStruct((parts, steps * half, size), jnp.float32),
        in_specs=[pl.BlockSpec(memory_space=pltpu.VMEM)],
        out_specs=pl.BlockSpec(memory_space=pl.ANY),
        scratch_shapes=[
            pltpu.VMEM((steps, parts, half, size), jnp.float32),
            pltpu.SemaphoreType.DMA((steps,)),
        ],
        compiler_params=pltpu.CompilerParams(vmem_limit_bytes=40 * 1024 * 1024),
        name="pairs",
    )(blocks.reshape(5, parts, size, samples))
    return out[None]


def solution(mesh):
    in_specs = (P(None, ("chan", "ablk"), None, None), P(None, ("chan", "ablk"), None))
    out_specs = P("chan", None, "ablk", None)
    return jax.shard_map(body, mesh=mesh, in_specs=in_specs, out_specs=out_specs, check_vma=False)
```

```python
import functools

import jax
import jax.numpy as jnp
from jax import lax
from jax.experimental import pallas as pl
from jax.experimental.pallas import tpu as pltpu
from jax.sharding import PartitionSpec as P

MESH = pl.DeviceIdType.MESH

SIDE = 4
PEERS = SIDE * SIDE
ROWS = 16
LANES = 128
OCTET = 8
GROUPS = 4
UPS = 4, 4, 6, 4
DELAY = 8
EARLY = 4


def wrap(i):
    return lax.rem(i + SIDE, SIDE)


def gather_kernel(
    volt, gain_hbm, blocks, diagonal, begun, raw, gain, cal, other, stash,
    raw_sem, gain_sem, block_sem, other_sem, stash_sem, twin_sem, send_sem,
):
    chan, ablk = lax.axis_index("chan"), lax.axis_index("ablk")
    x, y, parity = chan // 8, lax.rem(chan, 4), lax.rem(chan // 4, 2)
    group, core = ablk // 2, lax.rem(ablk, 2)
    size = blocks.shape[2] * ROWS
    scale = 1.0 / (4.0 * cal.shape[3])
    lane_tiles = cal.shape[3] // LANES
    step, pitch = OCTET * lane_tiles, raw.shape[2]
    flipped = 1 - parity
    xs = [8 * wrap(x + o) for o in range(SIDE)]
    ys = [wrap(y + o) for o in range(SIDE)]
    mine, theirs = 4 * parity, 4 * flipped
    me_c, flip_c = chan, xs[0] + ys[0] + theirs

    def place(i, p):
        return xs[i // SIDE] + ys[i % SIDE] + p

    ranks = [4 * wrap(x + o) for o in range(SIDE)]

    def rank(i):
        return ranks[i // SIDE] + ys[i % SIDE]

    def ups(distance):
        g = wrap(group + distance)
        count = jnp.where(g == 0, UPS[0], UPS[1])
        for k in range(2, GROUPS):
            count = jnp.where(g == k, UPS[k], count)
        return count

    def spared(distance):
        return core * jnp.where(wrap(group + distance) < 2, PEERS // 2, 0)

    up_own, up_below, up_next, up_after = ups(0), ups(-1), ups(1), ups(2)
    spared_next, spared_after = spared(1), spared(2)

    def rises(i, count):
        return i < count

    def along(distance, flip=False):
        return (flip_c if flip else chan), 2 * wrap(group + distance) + core

    twin_device = (chan, 2 * group + 1 - core)
    up, down = along(1), along(-1)
    home = flip_c, ablk
    far, onward, far_source = along(3 * parity - 1, True), along(1 - 2 * parity), along(3 * parity - 2, True)

    gain_copy = pltpu.make_async_copy(gain_hbm, gain, gain_sem)
    gain_copy.start()
    raw_copies = []
    for j in range(SIDE):
        target = wrap(x - j)
        raw_copies.append(pltpu.make_async_copy(volt.at[:, target], raw.at[j, :, pl.ds(0, step)], raw_sem.at[j]))
        raw_copies[-1].start()

    barrier = pltpu.get_barrier_semaphore()

    for to in [(place(i, mine), ablk) for i in range(1, PEERS)] + [up, down, home, far_source, twin_device]:
        pl.semaphore_signal(barrier, inc=1, device_id=to, device_id_type=MESH)

    def send(src, dst, kind, sem, to):
        pltpu.make_async_remote_copy(
            src_ref=src, dst_ref=dst, send_sem=send_sem.at[kind], recv_sem=sem, device_id=to, device_id_type=MESH
        ).start()

    def arrived(ref, sem):
        pltpu.make_async_copy(ref, ref, sem).wait()

    def share(slot, c, i):
        def go():
            to = slot - 1 + core
            sem = twin_sem.at[to, i // (PEERS // 2)]
            send(blocks.at[2 * slot, :, c], blocks.at[2 * to + 1, :, c], 2, sem, twin_device)

        if isinstance(slot, int) and slot == 1:
            go()
        else:
            pl.when((slot == 1) | (slot == 2 - 2 * core))(go)

    def direct(i):
        c = place(i, mine)
        own, across = blocks.at[0, :, c], other.at[:, i]
        if i == 0:
            own, across = cal.at[me_c], cal.at[flip_c]
        else:
            arrived(own, block_sem.at[0, i])
        rising = rises(i, up_own)

        @pl.when(rising)
        def _():
            send(own, stash.at[:, i], 3, stash_sem.at[i], up)

        @pl.when(jnp.logical_not(rising))
        def _():
            send(own, blocks.at[2, :, c], 3, block_sem.at[1, i], down)

        if i > 0:
            arrived(across, other_sem.at[i])
        send(across, blocks.at[2 + 2 * parity, :, c], 6, block_sem.at[1 + parity, PEERS + i], far)
        send(across, blocks.at[0, :, c], 5, block_sem.at[0, PEERS + i], home)
        if i == 0:
            arrived(blocks.at[0, :, c], block_sem.at[0, 0])
        share(0, c, i)

    def lift(i):
        @pl.when(rises(i, up_below))
        def _():
            arrived(stash.at[:, i], stash_sem.at[i])
            send(stash.at[:, i], blocks.at[4, :, place(i, mine)], 4, block_sem.at[2, i], up)

    first, second = 2 - parity, 1 + parity

    def relay(i):
        c, d = place(i, mine), place(i, theirs)
        arrived(blocks.at[2 * first, :, d], block_sem.at[first, PEERS + i])

        @pl.when((parity == 0) | (rank(i) >= spared_next))
        def _():
            send(blocks.at[2 * first, :, d], blocks.at[2 * second, :, d], 4, block_sem.at[second, PEERS + i], onward)

        share(first, d, i)
        arrived(blocks.at[0, :, d], block_sem.at[0, PEERS + i])
        share(0, d, i)

        @pl.when(jnp.logical_not(rises(i, up_next)))
        def _():
            arrived(blocks.at[2, :, c], block_sem.at[1, i])

            @pl.when(rank(i) >= spared_next)
            def _():
                send(blocks.at[2, :, c], blocks.at[4, :, c], 4, block_sem.at[2, i], down)

            share(1, c, i)

    def raised(i):
        c = place(i, mine)

        @pl.when(rises(i, up_after))
        def _():
            arrived(blocks.at[4, :, c], block_sem.at[2, i])
            send(blocks.at[4, :, c], blocks.at[2, :, c], 4, block_sem.at[1, i], up)
            share(2, c, i)

    gain_copy.wait()
    for j in range(SIDE):
        target = wrap(x - j)
        raw_copies[j].wait()
        octet = raw.at[j].reshape(2 * ROWS * pitch, LANES)
        gain_re, gain_im = gain[0, :, :OCTET], gain[1, :, :OCTET]
        for o in range(1, SIDE):
            gain_re = jnp.where(target == o, gain[0, :, o * OCTET : (o + 1) * OCTET], gain_re)
            gain_im = jnp.where(target == o, gain[1, :, o * OCTET : (o + 1) * OCTET], gain_im)
        for s in range(OCTET):
            g_re = jnp.broadcast_to(gain_re[:, s : s + 1], (ROWS, LANES))
            g_im = jnp.broadcast_to(gain_im[:, s : s + 1], (ROWS, LANES))
            f = target * OCTET + s
            for t in range(lane_tiles):
                start = t * OCTET + s
                v_re = octet[pl.ds(start, ROWS, stride=pitch), :].astype(jnp.float32)
                v_im = octet[pl.ds(ROWS * pitch + start, ROWS, stride=pitch), :].astype(jnp.float32)
                cal[f, 0, :, t * LANES : (t + 1) * LANES] = (g_re * v_re - g_im * v_im).astype(jnp.bfloat16)
                cal[f, 1, :, t * LANES : (t + 1) * LANES] = (g_re * v_im + g_im * v_re).astype(jnp.bfloat16)

        if j == 0:
            pl.semaphore_wait(barrier, PEERS + 4)
            pltpu.make_async_copy(cal.at[me_c], blocks.at[0, :, me_c], block_sem.at[0, 0]).start()

        for k in range(1 if j == 0 else 0, SIDE):
            i = j * SIDE + k
            c = 8 * target + wrap(y - k)
            send(cal.at[c + mine], blocks.at[0, :, me_c], 0, block_sem.at[0, i], (c + mine, ablk))
            send(cal.at[c + theirs], other.at[:, i], 1, other_sem.at[i], (c + mine, ablk))
        if j < EARLY:
            direct(j)

    for i in range(EARLY, PEERS + 2 * DELAY):
        if i < PEERS:
            direct(i)
        if 0 <= i - DELAY < PEERS:
            lift(i - DELAY)
            relay(i - DELAY)
        if i >= 2 * DELAY:
            raised(i - 2 * DELAY)

    def twin(q, side):
        ref = blocks.at[2 * q + 1, :, pl.ds(0, PEERS)]
        arrived(ref, twin_sem.at[q, side])

    def diagonal_part(part):
        columns = slice(part * size // 2, (part + 1) * size // 2)
        right = blocks[0, :, part * PEERS : (part + 1) * PEERS].reshape(2, size // 2, -1)
        diagonal[0, :, columns], diagonal[1, :, columns] = product(blocks[0].reshape(2, size, -1), right, scale)

    def slot_part(k):
        right = [blocks[k, :, pl.ds(xs[o], 8)].reshape(2, LANES, -1) for o in range(2)]
        made = product(blocks[0].reshape(2, size, -1), jnp.concatenate(right, axis=1), scale)
        for o in range(2):
            for part in range(2):
                begun[k - 1, o, part] = made[part][:, o * LANES : (o + 1) * LANES]

    for i in range(PEERS):
        c, d = place(i, mine), place(i, theirs)

        @pl.when((parity == 0) | (rank(i) >= spared_after))
        def _():
            arrived(blocks.at[2 * second, :, d], block_sem.at[second, PEERS + i])
            share(second, d, i)

        @pl.when(rises(i, up_next))
        def _():
            arrived(blocks.at[2, :, c], block_sem.at[1, i])
            share(1, c, i)

        @pl.when(jnp.logical_not(rises(i, up_after)) & (rank(i) >= spared_after))
        def _():
            arrived(blocks.at[4, :, c], block_sem.at[2, i])
            share(2, c, i)

    diagonal_part(0)
    diagonal_part(1)
    twin(0, 0)
    twin(1, 0)
    slot_part(2)
    slot_part(1)
    slot_part(3)

    def sent(kind, count):
        ref = blocks.at[0, :, pl.ds(0, count)]
        pltpu.make_async_copy(ref, ref, send_sem.at[kind]).wait()

    for kind, count in ((0, 15), (1, 15), (3, 16), (5, 16), (6, 16)):
        sent(kind, count)
    count = up_below + up_after + (PEERS - parity * spared_next)
    for i in range(PEERS):
        count = count + jnp.where(rises(i, up_next) | (rank(i) < spared_next), 0, 1)
    for bit in (1, 2, 4, 8, 16, 32):

        @pl.when(lax.rem(count // bit, 2) == 1)
        def _(bit=bit):
            sent(4, bit)

    pair = blocks.at[pl.ds(0, 2)]
    pltpu.make_async_copy(pair, pair, send_sem.at[2]).wait()
    twin(0, 1)
    twin(1, 1)


def product(left, right, scale):
    def dot(a, b):
        return lax.dot_general(a, b, (((1,), (1,)), ((), ())), preferred_element_type=jnp.float32)

    real = dot(left[0], right[0]) + dot(left[1], right[1])
    imag = dot(left[1], right[0]) - dot(left[0], right[1])
    return real * scale, imag * scale


def pairs_kernel(blocks, diagonal, begun, out, made, last, sem, *, scale):
    chan, ablk = lax.axis_index("chan"), lax.axis_index("ablk")
    size = diagonal.shape[1]
    half = size // 2

    def tile(k, o):
        return pl.ds(k * size, size), pl.ds(pl.multiple_of((chan // 8 + o) % SIDE * LANES, LANES), LANES)

    copies = []

    def put(src, *where):
        copies.append(pltpu.make_async_copy(src, out.at[:, *where], sem.at[len(copies)]))
        copies[-1].start()

    put(diagonal, pl.ds(0, size))
    for k in range(1, SIDE):
        for o in range(2):
            put(begun.at[k - 1, o], *tile(k, o))

    upper = ablk >= 4

    @pl.when(jnp.logical_not(upper))
    def _():
        last[0], last[1] = product(blocks[0, :, :half], blocks[4], scale)

    @pl.when(upper)
    def _():
        last[0], last[1] = product(blocks[4, :, half:], blocks[0], scale)

    put(last, pl.ds(SIDE * size, half))
    for k in range(1, SIDE):
        right = jnp.concatenate([blocks[k, :, tile(0, o)[1], :] for o in (2, 3)], axis=1)
        both = product(blocks[0], right, scale)
        for o in range(2):
            for part in range(2):
                made[k - 1, o, part] = both[part][:, o * LANES : (o + 1) * LANES]
            put(made.at[k - 1, o], *tile(k, 2 + o))
    for copy in copies:
        copy.wait()


def body(voltages, complex_gains):
    parts, rows, channels, samples = voltages.shape
    lane_tiles = samples // LANES
    octets = channels // OCTET
    tiles = voltages.reshape(parts, rows, octets, OCTET, lane_tiles, LANES).transpose(0, 1, 2, 4, 3, 5)
    tiles = tiles.reshape(parts * rows, octets, lane_tiles * OCTET, LANES)
    size = 32 * rows
    blocks, diagonal, begun = pl.pallas_call(
        gather_kernel,
        out_shape=(
            pltpu.VMEM((5, parts, 32, rows, samples), jnp.bfloat16),
            pltpu.VMEM((parts, size, size), jnp.float32),
            pltpu.VMEM((3, 2, parts, size, LANES), jnp.float32),
        ),
        in_specs=[pl.BlockSpec(memory_space=pltpu.HBM)] * 2,
        out_specs=(pl.BlockSpec(memory_space=pltpu.VMEM),) * 3,
        scratch_shapes=[
            pltpu.VMEM((octets, parts * rows, lane_tiles * OCTET + 8, LANES), jnp.int32),
            pltpu.VMEM((parts, rows, channels), jnp.float32),
            pltpu.VMEM((channels, parts, rows, samples), jnp.bfloat16),
            pltpu.VMEM((parts, PEERS, rows, samples), jnp.bfloat16),
            pltpu.VMEM((parts, PEERS, rows, samples), jnp.bfloat16),
            pltpu.SemaphoreType.DMA((SIDE,)),
            pltpu.SemaphoreType.DMA,
            pltpu.SemaphoreType.DMA((3, 2 * PEERS)),
            pltpu.SemaphoreType.DMA((PEERS,)),
            pltpu.SemaphoreType.DMA((PEERS,)),
            pltpu.SemaphoreType.DMA((2, 2)),
            pltpu.SemaphoreType.DMA((7,)),
        ],
        compiler_params=pltpu.CompilerParams(
            collective_id=0, has_side_effects=True, vmem_limit_bytes=40 * 1024 * 1024
        ),
        name="gather",
    )(*(pltpu.with_memory_space_constraint(a, pltpu.HBM) for a in (tiles, complex_gains)))

    out = pl.pallas_call(
        functools.partial(pairs_kernel, scale=1.0 / (4.0 * samples)),
        out_shape=jax.ShapeDtypeStruct((parts, 4 * size + size // 2, size), jnp.float32),
        in_specs=[pl.BlockSpec(memory_space=pltpu.VMEM)] * 3,
        out_specs=pl.BlockSpec(memory_space=pl.ANY),
        scratch_shapes=[
            pltpu.VMEM((3, 2, parts, size, LANES), jnp.float32),
            pltpu.VMEM((parts, size // 2, size), jnp.float32),
            pltpu.SemaphoreType.DMA((14,)),
        ],
        compiler_params=pltpu.CompilerParams(vmem_limit_bytes=40 * 1024 * 1024),
        name="pairs",
    )(blocks.reshape(5, parts, size, samples), diagonal, begun)
    return out[None]


def solution(mesh):
    in_specs = (P(None, ("chan", "ablk"), None, None), P(None, ("chan", "ablk"), None))
    out_specs = P("chan", None, "ablk", None)
    return jax.shard_map(body, mesh=mesh, in_specs=in_specs, out_specs=out_specs, check_vma=False)
```

```python
import functools

import jax
import jax.numpy as jnp
from jax import lax
from jax.experimental import pallas as pl
from jax.experimental.pallas import tpu as pltpu
from jax.sharding import PartitionSpec as P

MESH = pl.DeviceIdType.MESH

SIDE = 4
PEERS = SIDE * SIDE
ROWS = 16
LANES = 128
OCTET = 8
GROUPS = 4
UPS = 4, 4, 6, 4
DELAY = 10
EARLY = 4


def wrap(i):
    return lax.rem(i + SIDE, SIDE)


def gather_kernel(
    volt, gain_hbm, blocks, diagonal, begun, raw, gain, cal, other, stash,
    raw_sem, gain_sem, block_sem, other_sem, stash_sem, twin_sem, send_sem, column_sem,
):
    chan, ablk = lax.axis_index("chan"), lax.axis_index("ablk")
    x, y, parity = chan // 8, lax.rem(chan, 4), lax.rem(chan // 4, 2)
    group, core = ablk // 2, lax.rem(ablk, 2)
    size = blocks.shape[2] * ROWS
    scale = 1.0 / (4.0 * cal.shape[3])
    lane_tiles = cal.shape[3] // LANES
    step, pitch = OCTET * lane_tiles, raw.shape[2]
    flipped = 1 - parity
    xs = [8 * wrap(x + o) for o in range(SIDE)]
    ys = [wrap(y + o) for o in range(SIDE)]
    mine, theirs = 4 * parity, 4 * flipped
    me_c, flip_c = chan, xs[0] + ys[0] + theirs

    def place(i, p):
        return xs[i // SIDE] + ys[i % SIDE] + p

    ranks = [4 * wrap(x + o) for o in range(SIDE)]

    def rank(i):
        return ranks[i // SIDE] + ys[i % SIDE]

    def ups(distance):
        g = wrap(group + distance)
        count = jnp.where(g == 0, UPS[0], UPS[1])
        for k in range(2, GROUPS):
            count = jnp.where(g == k, UPS[k], count)
        return count

    def spared(distance):
        return core * jnp.where(wrap(group + distance) < 2, PEERS // 2, 0)

    up_own, up_below, up_next, up_after = ups(0), ups(-1), ups(1), ups(2)
    spared_next, spared_after = spared(1), spared(2)

    def rises(i, count):
        return i < count

    def along(distance, flip=False):
        return (flip_c if flip else chan), 2 * wrap(group + distance) + core

    twin_device = (chan, 2 * group + 1 - core)
    up, down = along(1), along(-1)
    home = flip_c, ablk
    far, onward, far_source = along(3 * parity - 1, True), along(1 - 2 * parity), along(3 * parity - 2, True)

    barrier = pltpu.get_barrier_semaphore()
    row = [(place(i, mine), ablk) for i in range(SIDE, PEERS, SIDE)]
    for to in [up, down, home, far_source, twin_device] + [(place(i, mine), ablk) for i in range(1, SIDE)] + row:
        pl.semaphore_signal(barrier, inc=1, device_id=to, device_id_type=MESH)

    gain_copy = pltpu.make_async_copy(gain_hbm, gain, gain_sem)
    gain_copy.start()
    raw_copies = []
    for j in range(SIDE):
        target = wrap(x - j)
        raw_copies.append(pltpu.make_async_copy(volt.at[:, target], raw.at[j, :, pl.ds(0, step)], raw_sem.at[j]))
        raw_copies[-1].start()

    def send(src, dst, kind, sem, to):
        pltpu.make_async_remote_copy(
            src_ref=src, dst_ref=dst, send_sem=send_sem.at[kind], recv_sem=sem, device_id=to, device_id_type=MESH
        ).start()

    def arrived(ref, sem):
        pltpu.make_async_copy(ref, ref, sem).wait()

    def share(slot, c, i):
        def go():
            to = slot - 1 + core
            sem = twin_sem.at[to, i // (PEERS // 2)]
            send(blocks.at[2 * slot, :, c], blocks.at[2 * to + 1, :, c], 2, sem, twin_device)

        if isinstance(slot, int) and slot == 1:
            go()
        else:
            pl.when((slot == 1) | (slot == 2 - 2 * core))(go)

    def direct(i):
        c = place(i, mine)
        own, across = blocks.at[0, :, c], other.at[:, i]
        if i == 0:
            own, across = cal.at[me_c], cal.at[flip_c]
        else:
            arrived(own, block_sem.at[0, i])
        rising = rises(i, up_own)

        @pl.when(rising)
        def _():
            send(own, stash.at[:, i], 3, stash_sem.at[i], up)

        @pl.when(jnp.logical_not(rising))
        def _():
            send(own, blocks.at[2, :, c], 3, block_sem.at[1, i], down)

        if i > 0:
            arrived(across, other_sem.at[i])
        send(across, blocks.at[2 + 2 * parity, :, c], 6, block_sem.at[1 + parity, PEERS + i], far)
        send(across, blocks.at[0, :, c], 5, block_sem.at[0, PEERS + i], home)
        if i == 0:
            arrived(blocks.at[0, :, c], block_sem.at[0, 0])
        share(0, c, i)

    def lift(i):
        @pl.when(rises(i, up_below))
        def _():
            arrived(stash.at[:, i], stash_sem.at[i])
            send(stash.at[:, i], blocks.at[4, :, place(i, mine)], 4, block_sem.at[2, i], up)

    first, second = 2 - parity, 1 + parity

    def relay(i):
        c, d = place(i, mine), place(i, theirs)
        arrived(blocks.at[2 * first, :, d], block_sem.at[first, PEERS + i])

        @pl.when((parity == 0) | (rank(i) >= spared_next))
        def _():
            send(blocks.at[2 * first, :, d], blocks.at[2 * second, :, d], 4, block_sem.at[second, PEERS + i], onward)

        share(first, d, i)
        arrived(blocks.at[0, :, d], block_sem.at[0, PEERS + i])
        share(0, d, i)

        @pl.when(jnp.logical_not(rises(i, up_next)))
        def _():
            arrived(blocks.at[2, :, c], block_sem.at[1, i])

            @pl.when(rank(i) >= spared_next)
            def _():
                send(blocks.at[2, :, c], blocks.at[4, :, c], 4, block_sem.at[2, i], down)

            share(1, c, i)

    def raised(i):
        c = place(i, mine)

        @pl.when(rises(i, up_after))
        def _():
            arrived(blocks.at[4, :, c], block_sem.at[2, i])
            send(blocks.at[4, :, c], blocks.at[2, :, c], 4, block_sem.at[1, i], up)
            share(2, c, i)

    gain_copy.wait()
    for j in range(SIDE):
        target = wrap(x - j)
        raw_copies[j].wait()
        octet = raw.at[j].reshape(2 * ROWS * pitch, LANES)
        gain_re, gain_im = gain[0, :, :OCTET], gain[1, :, :OCTET]
        for o in range(1, SIDE):
            gain_re = jnp.where(target == o, gain[0, :, o * OCTET : (o + 1) * OCTET], gain_re)
            gain_im = jnp.where(target == o, gain[1, :, o * OCTET : (o + 1) * OCTET], gain_im)
        for s in range(OCTET):
            g_re = jnp.broadcast_to(gain_re[:, s : s + 1], (ROWS, LANES))
            g_im = jnp.broadcast_to(gain_im[:, s : s + 1], (ROWS, LANES))
            f = target * OCTET + s
            for t in range(lane_tiles):
                start = t * OCTET + s
                v_re = octet[pl.ds(start, ROWS, stride=pitch), :].astype(jnp.float32)
                v_im = octet[pl.ds(ROWS * pitch + start, ROWS, stride=pitch), :].astype(jnp.float32)
                cal[f, 0, :, t * LANES : (t + 1) * LANES] = (g_re * v_re - g_im * v_im).astype(jnp.bfloat16)
                cal[f, 1, :, t * LANES : (t + 1) * LANES] = (g_re * v_im + g_im * v_re).astype(jnp.bfloat16)

        if j == 0:
            pl.semaphore_wait(barrier, 2 * (SIDE - 1) + 5)
            for to in row:
                pl.semaphore_signal(column_sem, inc=1, device_id=to, device_id_type=MESH)
            pltpu.make_async_copy(cal.at[me_c], blocks.at[0, :, me_c], block_sem.at[0, 0]).start()

        if j == 1:
            pl.semaphore_wait(column_sem, SIDE - 1)

        for k in range(1 if j == 0 else 0, SIDE):
            i = j * SIDE + k
            c = 8 * target + wrap(y - k)
            send(cal.at[c + mine], blocks.at[0, :, me_c], 0, block_sem.at[0, i], (c + mine, ablk))
            send(cal.at[c + theirs], other.at[:, i], 1, other_sem.at[i], (c + mine, ablk))
        if j < EARLY:
            direct(j)

    for i in range(EARLY, PEERS + 2 * DELAY):
        if i < PEERS:
            direct(i)
        if 0 <= i - DELAY < PEERS:
            lift(i - DELAY)
            relay(i - DELAY)
        if i >= 2 * DELAY:
            raised(i - 2 * DELAY)

    def twin(q, side):
        ref = blocks.at[2 * q + 1, :, pl.ds(0, PEERS)]
        arrived(ref, twin_sem.at[q, side])

    def diagonal_part(part):
        columns = slice(part * size // 2, (part + 1) * size // 2)
        right = blocks[0, :, part * PEERS : (part + 1) * PEERS].reshape(2, size // 2, -1)
        diagonal[0, :, columns], diagonal[1, :, columns] = product(blocks[0].reshape(2, size, -1), right, scale)

    def slot_part(k):
        right = [blocks[k, :, pl.ds(xs[o], 8)].reshape(2, LANES, -1) for o in range(2)]
        made = product(blocks[0].reshape(2, size, -1), jnp.concatenate(right, axis=1), scale)
        for o in range(2):
            for part in range(2):
                begun[k - 1, o, part] = made[part][:, o * LANES : (o + 1) * LANES]

    for i in range(PEERS):
        c, d = place(i, mine), place(i, theirs)

        @pl.when((parity == 0) | (rank(i) >= spared_after))
        def _():
            arrived(blocks.at[2 * second, :, d], block_sem.at[second, PEERS + i])
            share(second, d, i)

        @pl.when(rises(i, up_next))
        def _():
            arrived(blocks.at[2, :, c], block_sem.at[1, i])
            share(1, c, i)

        @pl.when(jnp.logical_not(rises(i, up_after)) & (rank(i) >= spared_after))
        def _():
            arrived(blocks.at[4, :, c], block_sem.at[2, i])
            share(2, c, i)

        if i in (0, 3):
            diagonal_part(i // 3)

    twin(0, 0)
    twin(1, 0)
    slot_part(2)
    slot_part(1)
    slot_part(3)

    def sent(kind, count):
        ref = blocks.at[0, :, pl.ds(0, count)]
        pltpu.make_async_copy(ref, ref, send_sem.at[kind]).wait()

    for kind, count in ((0, 15), (1, 15), (3, 16), (5, 16), (6, 16)):
        sent(kind, count)
    count = up_below + up_after + (PEERS - parity * spared_next)
    for i in range(PEERS):
        count = count + jnp.where(rises(i, up_next) | (rank(i) < spared_next), 0, 1)
    for bit in (1, 2, 4, 8, 16, 32):

        @pl.when(lax.rem(count // bit, 2) == 1)
        def _(bit=bit):
            sent(4, bit)

    pair = blocks.at[pl.ds(0, 2)]
    pltpu.make_async_copy(pair, pair, send_sem.at[2]).wait()
    twin(0, 1)
    twin(1, 1)


def product(left, right, scale):
    def dot(a, b):
        return lax.dot_general(a, b, (((1,), (1,)), ((), ())), preferred_element_type=jnp.float32)

    real = dot(left[0], right[0]) + dot(left[1], right[1])
    imag = dot(left[1], right[0]) - dot(left[0], right[1])
    return real * scale, imag * scale


def pairs_kernel(blocks, diagonal, begun, out, made, last, sem, *, scale):
    chan, ablk = lax.axis_index("chan"), lax.axis_index("ablk")
    size = diagonal.shape[1]
    half = size // 2

    def tile(k, o):
        return pl.ds(k * size, size), pl.ds(pl.multiple_of((chan // 8 + o) % SIDE * LANES, LANES), LANES)

    copies = []

    def put(src, *where):
        copies.append(pltpu.make_async_copy(src, out.at[:, *where], sem.at[len(copies)]))
        copies[-1].start()

    put(diagonal, pl.ds(0, size))
    for k in range(1, SIDE):
        for o in range(2):
            put(begun.at[k - 1, o], *tile(k, o))

    upper = ablk >= 4

    @pl.when(jnp.logical_not(upper))
    def _():
        last[0], last[1] = product(blocks[0, :, :half], blocks[4], scale)

    @pl.when(upper)
    def _():
        last[0], last[1] = product(blocks[4, :, half:], blocks[0], scale)

    put(last, pl.ds(SIDE * size, half))
    for k in range(1, SIDE):
        right = jnp.concatenate([blocks[k, :, tile(0, o)[1], :] for o in (2, 3)], axis=1)
        both = product(blocks[0], right, scale)
        for o in range(2):
            for part in range(2):
                made[k - 1, o, part] = both[part][:, o * LANES : (o + 1) * LANES]
            put(made.at[k - 1, o], *tile(k, 2 + o))
    for copy in copies:
        copy.wait()


def body(voltages, complex_gains):
    parts, rows, channels, samples = voltages.shape
    lane_tiles = samples // LANES
    octets = channels // OCTET
    tiles = voltages.reshape(parts, rows, octets, OCTET, lane_tiles, LANES).transpose(0, 1, 2, 4, 3, 5)
    tiles = tiles.reshape(parts * rows, octets, lane_tiles * OCTET, LANES)
    size = 32 * rows
    blocks, diagonal, begun = pl.pallas_call(
        gather_kernel,
        out_shape=(
            pltpu.VMEM((5, parts, 32, rows, samples), jnp.bfloat16),
            pltpu.VMEM((parts, size, size), jnp.float32),
            pltpu.VMEM((3, 2, parts, size, LANES), jnp.float32),
        ),
        in_specs=[pl.BlockSpec(memory_space=pltpu.HBM)] * 2,
        out_specs=(pl.BlockSpec(memory_space=pltpu.VMEM),) * 3,
        scratch_shapes=[
            pltpu.VMEM((octets, parts * rows, lane_tiles * OCTET + 8, LANES), jnp.int32),
            pltpu.VMEM((parts, rows, channels), jnp.float32),
            pltpu.VMEM((channels, parts, rows, samples), jnp.bfloat16),
            pltpu.VMEM((parts, PEERS, rows, samples), jnp.bfloat16),
            pltpu.VMEM((parts, PEERS, rows, samples), jnp.bfloat16),
            pltpu.SemaphoreType.DMA((SIDE,)),
            pltpu.SemaphoreType.DMA,
            pltpu.SemaphoreType.DMA((3, 2 * PEERS)),
            pltpu.SemaphoreType.DMA((PEERS,)),
            pltpu.SemaphoreType.DMA((PEERS,)),
            pltpu.SemaphoreType.DMA((2, 2)),
            pltpu.SemaphoreType.DMA((7,)),
            pltpu.SemaphoreType.REGULAR,
        ],
        compiler_params=pltpu.CompilerParams(
            collective_id=0, has_side_effects=True, vmem_limit_bytes=40 * 1024 * 1024
        ),
        name="gather",
    )(*(pltpu.with_memory_space_constraint(a, pltpu.HBM) for a in (tiles, complex_gains)))

    out = pl.pallas_call(
        functools.partial(pairs_kernel, scale=1.0 / (4.0 * samples)),
        out_shape=jax.ShapeDtypeStruct((parts, 4 * size + size // 2, size), jnp.float32),
        in_specs=[pl.BlockSpec(memory_space=pltpu.VMEM)] * 3,
        out_specs=pl.BlockSpec(memory_space=pl.ANY),
        scratch_shapes=[
            pltpu.VMEM((3, 2, parts, size, LANES), jnp.float32),
            pltpu.VMEM((parts, size // 2, size), jnp.float32),
            pltpu.SemaphoreType.DMA((14,)),
        ],
        compiler_params=pltpu.CompilerParams(vmem_limit_bytes=40 * 1024 * 1024),
        name="pairs",
    )(blocks.reshape(5, parts, size, samples), diagonal, begun)
    return out[None]


def solution(mesh):
    in_specs = (P(None, ("chan", "ablk"), None, None), P(None, ("chan", "ablk"), None))
    out_specs = P("chan", None, "ablk", None)
    return jax.shard_map(body, mesh=mesh, in_specs=in_specs, out_specs=out_specs, check_vma=False)
```

```python
import functools

import jax
import jax.numpy as jnp
from jax import lax
from jax.experimental import pallas as pl
from jax.experimental.pallas import tpu as pltpu
from jax.sharding import PartitionSpec as P

MESH = pl.DeviceIdType.MESH

SIDE = 4
PEERS = SIDE * SIDE
ROWS = 16
LANES = 128
OCTET = 8
GROUPS = 4
UPS = 4, 4, 6, 4
DELAY = 10
EARLY = 4


def wrap(i):
    return lax.rem(i + SIDE, SIDE)


def gather_kernel(
    volt, gain_hbm, blocks, diagonal, begun, raw, gain, cal, other, stash,
    raw_sem, gain_sem, block_sem, other_sem, stash_sem, twin_sem, send_sem, column_sem,
):
    chan, ablk = lax.axis_index("chan"), lax.axis_index("ablk")
    x, y, parity = chan // 8, lax.rem(chan, 4), lax.rem(chan // 4, 2)
    group, core = ablk // 2, lax.rem(ablk, 2)
    size = blocks.shape[2] * ROWS
    scale = 1.0 / (4.0 * cal.shape[3])
    lane_tiles = cal.shape[3] // LANES
    step, pitch = OCTET * lane_tiles, raw.shape[2]
    flipped = 1 - parity
    xs = [8 * wrap(x + o) for o in range(SIDE)]
    ys = [wrap(y + o) for o in range(SIDE)]
    mine, theirs = 4 * parity, 4 * flipped
    me_c, flip_c = chan, xs[0] + ys[0] + theirs

    def place(i, p):
        return xs[i // SIDE] + ys[i % SIDE] + p

    ranks = [4 * wrap(x + o) for o in range(SIDE)]

    def rank(i):
        return ranks[i // SIDE] + ys[i % SIDE]

    def ups(distance):
        g = wrap(group + distance)
        count = jnp.where(g == 0, UPS[0], UPS[1])
        for k in range(2, GROUPS):
            count = jnp.where(g == k, UPS[k], count)
        return count

    def spared(distance):
        return core * jnp.where(wrap(group + distance) < 2, PEERS // 2, 0)

    up_own, up_below, up_next, up_after = ups(0), ups(-1), ups(1), ups(2)
    spared_next, spared_after = spared(1), spared(2)

    def rises(i, count):
        return i < count

    def along(distance, flip=False):
        return (flip_c if flip else chan), 2 * wrap(group + distance) + core

    twin_device = (chan, 2 * group + 1 - core)
    up, down = along(1), along(-1)
    home = flip_c, ablk
    far, onward, far_source = along(3 * parity - 1, True), along(1 - 2 * parity), along(3 * parity - 2, True)

    barrier = pltpu.get_barrier_semaphore()
    row = [(place(i, mine), ablk) for i in range(SIDE, PEERS, SIDE)]
    for to in [up, down, home, far_source, twin_device] + [(place(i, mine), ablk) for i in range(1, SIDE)] + row:
        pl.semaphore_signal(barrier, inc=1, device_id=to, device_id_type=MESH)

    gain_copy = pltpu.make_async_copy(gain_hbm, gain, gain_sem)
    gain_copy.start()
    raw_copies = []
    for j in range(SIDE):
        target = wrap(x - j)
        raw_copies.append(pltpu.make_async_copy(volt.at[:, target], raw.at[j, :, pl.ds(0, step)], raw_sem.at[j]))
        raw_copies[-1].start()

    def send(src, dst, kind, sem, to):
        pltpu.make_async_remote_copy(
            src_ref=src, dst_ref=dst, send_sem=send_sem.at[kind], recv_sem=sem, device_id=to, device_id_type=MESH
        ).start()

    def arrived(ref, sem):
        pltpu.make_async_copy(ref, ref, sem).wait()

    def share(slot, c, i):
        def go():
            to = slot - 1 + core
            sem = twin_sem.at[to, i // (PEERS // 2)]
            send(blocks.at[2 * slot, :, c], blocks.at[2 * to + 1, :, c], 2, sem, twin_device)

        if isinstance(slot, int) and slot == 1:
            go()
        else:
            pl.when((slot == 1) | (slot == 2 - 2 * core))(go)

    def direct(i):
        c = place(i, mine)
        own, across = blocks.at[0, :, c], other.at[:, i]
        if i == 0:
            own, across = cal.at[me_c], cal.at[flip_c]
        else:
            arrived(own, block_sem.at[0, i])
        rising = rises(i, up_own)

        @pl.when(rising)
        def _():
            send(own, stash.at[:, i], 3, stash_sem.at[i], up)

        @pl.when(jnp.logical_not(rising))
        def _():
            send(own, blocks.at[2, :, c], 3, block_sem.at[1, i], down)

        if i > 0:
            arrived(across, other_sem.at[i])
        send(across, blocks.at[2 + 2 * parity, :, c], 6, block_sem.at[1 + parity, PEERS + i], far)
        send(across, blocks.at[0, :, c], 5, block_sem.at[0, PEERS + i], home)
        if i == 0:
            arrived(blocks.at[0, :, c], block_sem.at[0, 0])
        share(0, c, i)

    def lift(i):
        @pl.when(rises(i, up_below))
        def _():
            arrived(stash.at[:, i], stash_sem.at[i])
            send(stash.at[:, i], blocks.at[4, :, place(i, mine)], 4, block_sem.at[2, i], up)

    first, second = 2 - parity, 1 + parity

    def relay(i):
        c, d = place(i, mine), place(i, theirs)
        arrived(blocks.at[2 * first, :, d], block_sem.at[first, PEERS + i])

        @pl.when((parity == 0) | (rank(i) >= spared_next))
        def _():
            send(blocks.at[2 * first, :, d], blocks.at[2 * second, :, d], 4, block_sem.at[second, PEERS + i], onward)

        share(first, d, i)
        arrived(blocks.at[0, :, d], block_sem.at[0, PEERS + i])
        share(0, d, i)

        @pl.when(jnp.logical_not(rises(i, up_next)))
        def _():
            arrived(blocks.at[2, :, c], block_sem.at[1, i])

            @pl.when(rank(i) >= spared_next)
            def _():
                send(blocks.at[2, :, c], blocks.at[4, :, c], 4, block_sem.at[2, i], down)

            share(1, c, i)

    def raised(i):
        c = place(i, mine)

        @pl.when(rises(i, up_after))
        def _():
            arrived(blocks.at[4, :, c], block_sem.at[2, i])
            send(blocks.at[4, :, c], blocks.at[2, :, c], 4, block_sem.at[1, i], up)
            share(2, c, i)

    gain_copy.wait()
    for j in range(SIDE):
        target = wrap(x - j)
        raw_copies[j].wait()
        octet = raw.at[j].reshape(2 * ROWS * pitch, LANES)
        gain_re, gain_im = gain[0, :, :OCTET], gain[1, :, :OCTET]
        for o in range(1, SIDE):
            gain_re = jnp.where(target == o, gain[0, :, o * OCTET : (o + 1) * OCTET], gain_re)
            gain_im = jnp.where(target == o, gain[1, :, o * OCTET : (o + 1) * OCTET], gain_im)
        for s in range(OCTET):
            g_re = jnp.broadcast_to(gain_re[:, s : s + 1], (ROWS, LANES))
            g_im = jnp.broadcast_to(gain_im[:, s : s + 1], (ROWS, LANES))
            f = target * OCTET + s
            for t in range(lane_tiles):
                start = t * OCTET + s
                v_re = octet[pl.ds(start, ROWS, stride=pitch), :].astype(jnp.float32)
                v_im = octet[pl.ds(ROWS * pitch + start, ROWS, stride=pitch), :].astype(jnp.float32)
                cal[f, 0, :, t * LANES : (t + 1) * LANES] = (g_re * v_re - g_im * v_im).astype(jnp.bfloat16)
                cal[f, 1, :, t * LANES : (t + 1) * LANES] = (g_re * v_im + g_im * v_re).astype(jnp.bfloat16)

        if j == 0:
            pl.semaphore_wait(barrier, 2 * (SIDE - 1) + 5)
            for to in row:
                pl.semaphore_signal(column_sem, inc=1, device_id=to, device_id_type=MESH)
            pltpu.make_async_copy(cal.at[me_c], blocks.at[0, :, me_c], block_sem.at[0, 0]).start()

        if j == 1:
            pl.semaphore_wait(column_sem, SIDE - 1)

        for k in range(1 if j == 0 else 0, SIDE):
            i = j * SIDE + k
            c = 8 * target + wrap(y - k)
            send(cal.at[c + mine], blocks.at[0, :, me_c], 0, block_sem.at[0, i], (c + mine, ablk))
            send(cal.at[c + theirs], other.at[:, i], 1, other_sem.at[i], (c + mine, ablk))
        if j < EARLY:
            direct(j)

    for i in range(EARLY, PEERS + 2 * DELAY):
        if i < PEERS:
            direct(i)
        if 0 <= i - DELAY < PEERS:
            lift(i - DELAY)
            relay(i - DELAY)
        if i >= 2 * DELAY:
            raised(i - 2 * DELAY)

    def twin(q, side):
        ref = blocks.at[2 * q + 1, :, pl.ds(0, PEERS)]
        arrived(ref, twin_sem.at[q, side])

    def diagonal_part(part):
        columns = slice(part * size // 2, (part + 1) * size // 2)
        right = blocks[0, :, part * PEERS : (part + 1) * PEERS].reshape(2, size // 2, -1)
        diagonal[0, :, columns], diagonal[1, :, columns] = product(blocks[0].reshape(2, size, -1), right, scale)

    def slot_part(k):
        right = [blocks[k, :, pl.ds(xs[o], 8)].reshape(2, LANES, -1) for o in range(2)]
        made = product(blocks[0].reshape(2, size, -1), jnp.concatenate(right, axis=1), scale)
        for o in range(2):
            for part in range(2):
                begun[k - 1, o, part] = made[part][:, o * LANES : (o + 1) * LANES]

    for i in range(PEERS):
        c, d = place(i, mine), place(i, theirs)

        @pl.when((parity == 0) | (rank(i) >= spared_after))
        def _():
            arrived(blocks.at[2 * second, :, d], block_sem.at[second, PEERS + i])
            share(second, d, i)

        @pl.when(rises(i, up_next))
        def _():
            arrived(blocks.at[2, :, c], block_sem.at[1, i])
            share(1, c, i)

        @pl.when(jnp.logical_not(rises(i, up_after)) & (rank(i) >= spared_after))
        def _():
            arrived(blocks.at[4, :, c], block_sem.at[2, i])
            share(2, c, i)

        if i in (0, 3):
            diagonal_part(i // 3)
        elif i == 8:
            slot_part(2)

    twin(0, 0)
    twin(1, 0)
    slot_part(1)
    slot_part(3)

    def sent(kind, count):
        ref = blocks.at[0, :, pl.ds(0, count)]
        pltpu.make_async_copy(ref, ref, send_sem.at[kind]).wait()

    for kind, count in ((0, 15), (1, 15), (3, 16), (5, 16), (6, 16)):
        sent(kind, count)
    count = up_below + up_after + (PEERS - parity * spared_next)
    for i in range(PEERS):
        count = count + jnp.where(rises(i, up_next) | (rank(i) < spared_next), 0, 1)
    for bit in (1, 2, 4, 8, 16, 32):

        @pl.when(lax.rem(count // bit, 2) == 1)
        def _(bit=bit):
            sent(4, bit)

    pair = blocks.at[pl.ds(0, 2)]
    pltpu.make_async_copy(pair, pair, send_sem.at[2]).wait()
    twin(0, 1)
    twin(1, 1)


def product(left, right, scale):
    def dot(a, b):
        return lax.dot_general(a, b, (((1,), (1,)), ((), ())), preferred_element_type=jnp.float32)

    real = dot(left[0], right[0]) + dot(left[1], right[1])
    imag = dot(left[1], right[0]) - dot(left[0], right[1])
    return real * scale, imag * scale


def pairs_kernel(blocks, diagonal, begun, out, made, last, sem, *, scale):
    chan, ablk = lax.axis_index("chan"), lax.axis_index("ablk")
    size = diagonal.shape[1]
    half = size // 2

    def tile(k, o):
        return pl.ds(k * size, size), pl.ds(pl.multiple_of((chan // 8 + o) % SIDE * LANES, LANES), LANES)

    copies = []

    def put(src, *where):
        copies.append(pltpu.make_async_copy(src, out.at[:, *where], sem.at[len(copies)]))
        copies[-1].start()

    put(diagonal, pl.ds(0, size))
    for k in range(1, SIDE):
        for o in range(2):
            put(begun.at[k - 1, o], *tile(k, o))

    upper = ablk >= 4

    @pl.when(jnp.logical_not(upper))
    def _():
        last[0], last[1] = product(blocks[0, :, :half], blocks[4], scale)

    @pl.when(upper)
    def _():
        last[0], last[1] = product(blocks[4, :, half:], blocks[0], scale)

    put(last, pl.ds(SIDE * size, half))
    for k in range(1, SIDE):
        right = jnp.concatenate([blocks[k, :, tile(0, o)[1], :] for o in (2, 3)], axis=1)
        both = product(blocks[0], right, scale)
        for o in range(2):
            for part in range(2):
                made[k - 1, o, part] = both[part][:, o * LANES : (o + 1) * LANES]
            put(made.at[k - 1, o], *tile(k, 2 + o))
    for copy in copies:
        copy.wait()


def body(voltages, complex_gains):
    parts, rows, channels, samples = voltages.shape
    lane_tiles = samples // LANES
    octets = channels // OCTET
    tiles = voltages.reshape(parts, rows, octets, OCTET, lane_tiles, LANES).transpose(0, 1, 2, 4, 3, 5)
    tiles = tiles.reshape(parts * rows, octets, lane_tiles * OCTET, LANES)
    size = 32 * rows
    blocks, diagonal, begun = pl.pallas_call(
        gather_kernel,
        out_shape=(
            pltpu.VMEM((5, parts, 32, rows, samples), jnp.bfloat16),
            pltpu.VMEM((parts, size, size), jnp.float32),
            pltpu.VMEM((3, 2, parts, size, LANES), jnp.float32),
        ),
        in_specs=[pl.BlockSpec(memory_space=pltpu.HBM)] * 2,
        out_specs=(pl.BlockSpec(memory_space=pltpu.VMEM),) * 3,
        scratch_shapes=[
            pltpu.VMEM((octets, parts * rows, lane_tiles * OCTET + 8, LANES), jnp.int32),
            pltpu.VMEM((parts, rows, channels), jnp.float32),
            pltpu.VMEM((channels, parts, rows, samples), jnp.bfloat16),
            pltpu.VMEM((parts, PEERS, rows, samples), jnp.bfloat16),
            pltpu.VMEM((parts, PEERS, rows, samples), jnp.bfloat16),
            pltpu.SemaphoreType.DMA((SIDE,)),
            pltpu.SemaphoreType.DMA,
            pltpu.SemaphoreType.DMA((3, 2 * PEERS)),
            pltpu.SemaphoreType.DMA((PEERS,)),
            pltpu.SemaphoreType.DMA((PEERS,)),
            pltpu.SemaphoreType.DMA((2, 2)),
            pltpu.SemaphoreType.DMA((7,)),
            pltpu.SemaphoreType.REGULAR,
        ],
        compiler_params=pltpu.CompilerParams(
            collective_id=0, has_side_effects=True, vmem_limit_bytes=40 * 1024 * 1024
        ),
        name="gather",
    )(*(pltpu.with_memory_space_constraint(a, pltpu.HBM) for a in (tiles, complex_gains)))

    out = pl.pallas_call(
        functools.partial(pairs_kernel, scale=1.0 / (4.0 * samples)),
        out_shape=jax.ShapeDtypeStruct((parts, 4 * size + size // 2, size), jnp.float32),
        in_specs=[pl.BlockSpec(memory_space=pltpu.VMEM)] * 3,
        out_specs=pl.BlockSpec(memory_space=pl.ANY),
        scratch_shapes=[
            pltpu.VMEM((3, 2, parts, size, LANES), jnp.float32),
            pltpu.VMEM((parts, size // 2, size), jnp.float32),
            pltpu.SemaphoreType.DMA((14,)),
        ],
        compiler_params=pltpu.CompilerParams(vmem_limit_bytes=40 * 1024 * 1024),
        name="pairs",
    )(blocks.reshape(5, parts, size, samples), diagonal, begun)
    return out[None]


def solution(mesh):
    in_specs = (P(None, ("chan", "ablk"), None, None), P(None, ("chan", "ablk"), None))
    out_specs = P("chan", None, "ablk", None)
    return jax.shard_map(body, mesh=mesh, in_specs=in_specs, out_specs=out_specs, check_vma=False)
```
